32 devices in a mesh: head: 4 (over x, core), seq: 8 (over z, y).
Axes of the slice: x: 2, y: 2, z: 4, core: 2. Of those that a mesh axis runs over, the one named last changes fastest.
Arguments:
- queries: bfloat16 [4, 1024, 3584], P('head', 'seq'), may hold values from -16 to 16
- trunk_keys: bfloat16 [1024, 512], P('seq', 'head'), may hold values from -16 to 16
- trunk_values: bfloat16 [1024, 512], P('seq', 'head'), may hold values from -6 to 6
- out_grad: bfloat16 [4, 1024, 3584], P('head', 'seq'), may hold values from -6 to 6
- segment_ids: int32 [1024], P('seq'), may hold values from 0 to 3, never falling along the last dimension, each value on 1 to 512 neighbouring positions
Outputs:
- attended: bfloat16 [4, 1024, 3584], P('head', 'seq')
- query_grad: bfloat16 [4, 1024, 3584], P('head', 'seq')
- key_grad: float32 [1024, 512], P('seq', 'head')
- value_grad: float32 [1024, 512], P('seq', 'head')
The draws below stay inside these ranges and needn't reach their ends.
Inputs may be any that keep to these rules, and one draw needn't show every extreme that they name: `segment_ids`: documents are runs of consecutive tokens; one has exactly 512 tokens and none has more.
All inputs are finite; a program needn't handle non-finite values.
Results may differ from the reference program's by a relative error of at most 0.012.
Values may be sent and summed in bfloat16 or wider, within the bound.
A program may use at most 64 MiB of HBM per device.

```python
import math
import jax
import jax.numpy as jnp
import numpy as np
from jax import lax

DH = 128
QH = 28
KVH = 4
TOK_DEV = 128
SPAN = 4
MTP = 4
TOKENS = 1024
DOC_MOST = 512
DOCS = 4


def draw_queries(key, part):
    key = jax.random.fold_in(key, 3)
    base = jax.random.normal(key, (MTP, TOKENS, QH * DH), jnp.float32)
    return jnp.clip(base, -16.0, 16.0).astype(jnp.bfloat16)


def draw_trunk_keys(key, part):
    key = jax.random.fold_in(key, 5)
    base = jax.random.normal(key, (TOKENS, KVH * DH), jnp.float32)
    return jnp.clip(base, -16.0, 16.0).astype(jnp.bfloat16)


def steps_of(key, dims, cuts, least, largest):
    loudness = 1.0
    for axis_at, shards_of in cuts:
        heights = jax.random.uniform(jax.random.fold_in(jax.random.fold_in(key, 6), axis_at), (shards_of,), jnp.float32, least / len(cuts), largest / len(cuts))
        loudness = loudness * jnp.repeat(jnp.exp(heights), dims[axis_at] // shards_of).reshape((-1,) + (1,) * (len(dims) - 1 - axis_at))
    return loudness


def split_up(amount, total, bound, slope):
    loads = [(1 << 20) // math.isqrt(grade ** slope) + 1 for grade in range(2, amount + 1)]
    surplus, given = total - bound - (amount - 1), [1] * (amount - 1)
    while surplus > 0:
        free = [i for i in range(amount - 1) if given[i] < bound]
        whole, budget = sum([loads[i] for i in free]), surplus
        for i in free:
            extra = min(bound - given[i], max(1, budget * loads[i] // whole), surplus)
            given[i] = given[i] + extra
            surplus = surplus - extra
    return np.array([bound] + given)


def ragged_sizes(own_key, count, total, bound, skew):
    if count == 2:
        one = jax.random.randint(own_key, (), max(1, total - bound), min(bound, total - 1) + 1)
        return jnp.stack([one, total - one])
    lengths = jnp.asarray(split_up(count, total, bound, skew), jnp.int32)
    couples = (count - 1) // 2
    donor, taker = lengths[1:1 + 2 * couples:2], lengths[2:2 + 2 * couples:2]
    slack = jnp.minimum(donor - 1, bound - taker)
    passed = jax.random.randint(jax.random.fold_in(own_key, 1), (couples,), 0, 1 << 20) % (slack + 1)
    lengths = lengths.at[1:1 + 2 * couples:2].set(donor - passed).at[2:2 + 2 * couples:2].set(taker + passed)
    return lengths[jax.random.permutation(jax.random.fold_in(own_key, 2), count)]


def scatter_about(rng, extent, deviation, most, split=(), kind=jnp.bfloat16):
    array = jax.random.normal(rng, extent, jnp.float32) * deviation
    if len(split) > 0:
        array = steps_of(rng, extent, split, -0.22, 0.18) * array
    return jnp.clip(array, min=-most, max=most).astype(kind)


def setup_inputs(seed: int = 0) -> dict:
    splits = jax.random.split(jax.random.key(seed), 6)
    queries = draw_queries(jax.random.fold_in(splits[5], 71), 0)
    trunk_keys = draw_trunk_keys(jax.random.fold_in(splits[5], 71), 0)
    trunk_values = scatter_about(splits[2], (TOKENS, KVH * DH), 1.0, 6.0, ((0, 8), (1, 4)))
    out_grad = scatter_about(splits[3], (MTP, TOKENS, QH * DH), 1.0, 6.0, ((0, 4), (1, 8)))
    segment_ids = jnp.searchsorted(jnp.cumsum(ragged_sizes(splits[4], DOCS, TOKENS, DOC_MOST, 2)), jnp.arange(TOKENS), side="right").astype(jnp.int32)
    return dict(queries=queries, trunk_keys=trunk_keys, trunk_values=trunk_values, out_grad=out_grad, segment_ids=segment_ids)


def reference(queries, trunk_keys, trunk_values, out_grad, segment_ids):
    block_rows = TOK_DEV
    padding = SPAN * block_rows
    window = padding + block_rows
    q_group = QH // KVH
    scaling = 1.0 / math.sqrt(DH)
    keys_pad = jnp.concatenate([jnp.zeros((padding, KVH * DH), trunk_keys.dtype), trunk_keys], 0)
    values_pad = jnp.concatenate([jnp.zeros((padding, KVH * DH), trunk_values.dtype), trunk_values], 0)
    seg_pad = jnp.concatenate([jnp.full((padding,), -1, jnp.int32), segment_ids.astype(jnp.int32)], 0)

    def one_block(carried, block_index):
        key_acc, value_acc = carried
        block_start = (block_index * block_rows).astype(jnp.int32)
        query_blk = lax.dynamic_slice_in_dim(queries, block_start, block_rows, 1).astype(jnp.float32)
        query_blk = query_blk.reshape(MTP, block_rows, KVH, q_group, DH)
        grad_blk = lax.dynamic_slice_in_dim(out_grad, block_start, block_rows, 1).astype(jnp.float32)
        grad_blk = grad_blk.reshape(MTP, block_rows, KVH, q_group, DH)
        key_blk = lax.dynamic_slice_in_dim(keys_pad, block_start, window, 0).astype(jnp.float32).reshape(window, KVH, DH)
        value_blk = lax.dynamic_slice_in_dim(values_pad, block_start, window, 0).astype(jnp.float32).reshape(window, KVH, DH)
        seg_query = lax.dynamic_slice_in_dim(segment_ids.astype(jnp.int32), block_start, block_rows, 0)
        seg_key = lax.dynamic_slice_in_dim(seg_pad, block_start, window, 0)
        pos_query = block_start + jnp.arange(block_rows, dtype=jnp.int32)
        pos_key = block_start - padding + jnp.arange(window, dtype=jnp.int32)
        allowed = (seg_key[None, :] == seg_query[:, None]) & (pos_key[None, :] <= pos_query[:, None])
        scores = jnp.einsum('migrd,jgd->mgrij', query_blk, key_blk) * scaling
        scores = jnp.where(allowed[None, None, None], scores, -1e+30)
        row_top = lax.optimization_barrier(jnp.max(scores, axis=-1, keepdims=True))
        expd = jnp.exp(scores - row_top)
        probs = expd / lax.optimization_barrier(jnp.sum(expd, axis=-1, keepdims=True))
        probs_b = lax.optimization_barrier(probs.astype(jnp.bfloat16)).astype(jnp.float32)
        out32 = jnp.einsum('mgrij,jgd->migrd', probs_b, value_blk)
        delta_rows = jnp.transpose(lax.optimization_barrier(jnp.sum(grad_blk * out32, axis=-1)), (0, 2, 3, 1))
        dprobs = jnp.einsum('migrd,jgd->mgrij', grad_blk, value_blk)
        dscores = probs * (dprobs - delta_rows[..., None])
        dscores_b = lax.optimization_barrier(dscores.astype(jnp.bfloat16)).astype(jnp.float32)
        query_part = jnp.einsum('mgrij,jgd->migrd', dscores_b, key_blk) * scaling
        key_part = jnp.einsum('mgrij,migrd->jgd', dscores_b, query_blk) * scaling
        value_part = jnp.einsum('mgrij,migrd->jgd', probs_b, grad_blk)
        old_keys = lax.dynamic_slice_in_dim(key_acc, block_start, window, 0)
        key_acc = lax.dynamic_update_slice_in_dim(key_acc, old_keys + key_part.reshape(window, KVH * DH), block_start, 0)
        old_values = lax.dynamic_slice_in_dim(value_acc, block_start, window, 0)
        value_acc = lax.dynamic_update_slice_in_dim(value_acc, old_values + value_part.reshape(window, KVH * DH), block_start, 0)
        attended_blk = out32.reshape(MTP, block_rows, QH * DH).astype(jnp.bfloat16)
        query_grad_blk = query_part.reshape(MTP, block_rows, QH * DH).astype(jnp.bfloat16)
        return ((key_acc, value_acc), (attended_blk, query_grad_blk))
    zeros_acc = jnp.zeros((TOKENS + padding, KVH * DH), jnp.float32)
    (key_acc, value_acc), (attended_all, query_all) = lax.scan(one_block, (zeros_acc, zeros_acc), jnp.arange(TOKENS // block_rows, dtype=jnp.int32))
    attended = jnp.transpose(attended_all, (1, 0, 2, 3)).reshape(MTP, TOKENS, QH * DH)
    query_grad = jnp.transpose(query_all, (1, 0, 2, 3)).reshape(MTP, TOKENS, QH * DH)
    return (attended, query_grad, key_acc[padding:], value_acc[padding:])
```

```python
import functools
import math

import jax
import jax.numpy as jnp
from jax import lax
from jax.experimental import pallas as pl
from jax.experimental.pallas import tpu as pltpu
from jax.sharding import PartitionSpec as P

DH = 128
SPAN = 4
HOPS = SPAN + 1
BLOCK_ORDER = (1, 2, 3, 0, 4)
MESH = pl.DeviceIdType.MESH
NT = (((1,), (1,)), ((), ()))
NN = (((1,), (0,)), ((), ()))
TN = (((0,), (0,)), ((), ()))


def dot(a, b, dims):
    return lax.dot_general(a, b, dims, preferred_element_type=jnp.float32)


def kernel(
    seq_count, heads, group_size,
    q_hbm, k_ref, v_ref, g_hbm, seg_ref,
    out_hbm, dq_hbm, dk_ref, dv_ref,
    kv, qbuf, gbuf, obuf, dqbuf, kc, vc, bias, pscr, dscr,
    grad_own, grad_send, grad_recv, seq_send, seq_recv,
    in_sem, out_sem, kv_recv, kv_seq_send, kv_head_send,
    gr_send, gr_recv, sq_send, sq_recv,
):
    m = lax.axis_index("head")
    s = lax.axis_index("seq")
    rows = k_ref.shape[0]
    slab = group_size * DH
    scaling = 1.0 / math.sqrt(DH)
    core_peer = m + 1 - 2 * (m % 2)
    x_peer = (m + 2) % heads
    both_peer = (core_peer + 2) % heads
    groups = (m, core_peer, x_peer, both_peer)

    def columns(slot):
        return pl.ds(pl.multiple_of(groups[slot] * slab, DH), slab)

    def load(slot, which):
        src, dst = ((q_hbm, qbuf), (g_hbm, gbuf))[which]
        return pltpu.make_async_copy(
            src.at[0, :, columns(slot)], dst.at[slot], in_sem.at[which, slot])

    def store(slot, which):
        src, dst = ((obuf, out_hbm), (dqbuf, dq_hbm))[which]
        return pltpu.make_async_copy(
            src.at[slot], dst.at[0, :, columns(slot)], out_sem.at[which, slot])

    def remote(src, dst, send, recv, head, seq):
        return pltpu.make_async_remote_copy(
            src_ref=src, dst_ref=dst, send_sem=send, recv_sem=recv,
            device_id=(head, seq), device_id_type=MESH)

    def kv_seq(src_hop, dst_hop):
        return remote(kv.at[0, src_hop], kv.at[0, dst_hop], kv_seq_send.at[dst_hop],
                      kv_recv.at[0, dst_hop], m, s + (dst_hop - src_hop))

    def kv_head(slot, hop):
        src = kv.at[2 if slot == 3 else 0, hop]
        return remote(src, kv.at[slot, hop], kv_head_send.at[slot, hop],
                      kv_recv.at[slot, hop], x_peer if slot == 2 else core_peer, s)

    def kv_arrived(slot, hop):
        kv_head(slot, hop).wait_recv()

    for slot in (0, 1, 2, 3):
        load(slot, 0).start()
        load(slot, 1).start()

    kv[0, 0, 0:rows, :] = k_ref[...]
    kv[0, 0, rows:2 * rows, :] = v_ref[...]
    kv[0, 0, 2 * rows:, :] = jnp.broadcast_to(
        seg_ref[...].astype(jnp.float32), (16, rows)).astype(jnp.bfloat16)

    barrier = pltpu.get_barrier_semaphore()
    for peer in (core_peer, x_peer):
        pl.semaphore_signal(barrier, inc=1, device_id=(peer, s), device_id_type=MESH)
    expected = 2
    for step in (-2, -1, 1, 2):
        valid = (s >= -step) if step < 0 else (s < seq_count - step)

        @pl.when(valid)
        def _(step=step):
            pl.semaphore_signal(barrier, inc=1, device_id=(m, s + step), device_id_type=MESH)
        expected = expected + jnp.where(valid, 1, 0)
    pl.semaphore_wait(barrier, expected)

    for hop in (1, 2):
        @pl.when(s < seq_count - hop)
        def _(hop=hop):
            kv_seq(0, hop).start()
    kv_head(2, 0).start()
    kv_head(1, 0).start()

    for hop in range(1, HOPS):
        src_hop = hop if hop <= 2 else hop - 2

        @pl.when(s < hop)
        def _(hop=hop):
            kv[0, hop, 0:2 * rows, :] = jnp.zeros((2 * rows, DH), jnp.bfloat16)
            kv[0, hop, 2 * rows:, :] = jnp.full((16, DH), -1.0, jnp.bfloat16)

        @pl.when(s >= hop)
        def _(hop=hop):
            kv_seq(0 if hop <= 2 else hop - 2, hop).wait_recv()

        if hop <= 2:
            @pl.when((s >= hop) & (s < seq_count - 2))
            def _(hop=hop):
                kv_seq(hop, hop + 2).start()
        kv_head(2, hop).start()
        kv_head(1, hop).start()
        if hop >= 3:
            kv_arrived(2, hop - 3)
            kv_head(3, hop - 3).start()

    row_id = lax.broadcasted_iota(jnp.int32, (rows, rows), 0)
    col_id = lax.broadcasted_iota(jnp.int32, (rows, rows), 1)
    tri = col_id <= row_id

    def seg_row(hop):
        full = kv[0, hop, 2 * rows:, :].astype(jnp.float32)
        return full[0:1, :]

    seg_q = jnp.sum(jnp.where(row_id == col_id, seg_row(0), 0.0), axis=1, keepdims=True)
    for at, hop in enumerate((1, 2, 3)):
        bias[:, at * rows:(at + 1) * rows] = jnp.where(seg_row(hop) == seg_q, 0.0, -1e30)
    bias[:, 3 * rows:] = jnp.where(
        jnp.where(tri, seg_row(0), seg_row(4)) == seg_q, 0.0, -1e30)

    shared = 3 * rows

    def fold(x):
        edge = jnp.where(tri, x[:, shared:shared + rows], x[:, shared + rows:])
        return jnp.concatenate([x[:, :shared], edge], axis=1)

    def unfold(x):
        edge = x[:, shared:]
        zero = jnp.zeros_like(edge)
        return jnp.concatenate(
            [x[:, :shared], jnp.where(tri, edge, zero), jnp.where(tri, zero, edge)],
            axis=1).astype(jnp.bfloat16)

    def compute(slot):
        load(slot, 0).wait()
        load(slot, 1).wait()
        for at, hop in enumerate(BLOCK_ORDER):
            kc[at * rows:(at + 1) * rows, :] = kv[slot, hop, 0:rows, :]
            vc[at * rows:(at + 1) * rows, :] = kv[slot, hop, rows:2 * rows, :]

        for r in range(group_size):
            cols = slice(r * DH, (r + 1) * DH)
            q = qbuf[slot, :, cols]
            g = gbuf[slot, :, cols]
            t = fold(dot(q, kc[...], NT)) * (scaling * math.log2(math.e)) + bias[...]
            e = jnp.exp2(t - jnp.max(t, axis=1, keepdims=True))
            probs = e * (1.0 / jnp.sum(e, axis=1, keepdims=True))
            probs_b = unfold(probs)
            pscr[r * rows:(r + 1) * rows, :] = probs_b
            out32 = dot(probs_b, vc[...], NN)
            obuf[slot, :, cols] = out32.astype(jnp.bfloat16)
            delta = jnp.sum(g.astype(jnp.float32) * out32, axis=1, keepdims=True)
            dprobs = fold(dot(g, vc[...], NT))
            dscores_b = unfold(probs * (dprobs - delta))
            dscr[r * rows:(r + 1) * rows, :] = dscores_b
            dqbuf[slot, :, cols] = (dot(dscores_b, kc[...], NN) * scaling).astype(jnp.bfloat16)
        store(slot, 0).start()
        store(slot, 1).start()
        q_rows = jnp.concatenate(
            [qbuf[slot, :, r * DH:(r + 1) * DH] for r in range(group_size)], axis=0)
        g_rows = jnp.concatenate(
            [gbuf[slot, :, r * DH:(r + 1) * DH] for r in range(group_size)], axis=0)
        key_t = dot(q_rows, dscr[...], TN) * scaling
        value_t = dot(g_rows, pscr[...], TN)
        for at, hop in enumerate(BLOCK_ORDER):
            cols = slice(at * rows, (at + 1) * rows)
            if slot == 0:
                grad_own[hop, 0:DH, :] = key_t[:, cols]
                grad_own[hop, DH:, :] = value_t[:, cols]
            else:
                grad_send[slot - 1, hop, 0:DH, :] = key_t[:, cols].astype(jnp.bfloat16)
                grad_send[slot - 1, hop, DH:, :] = value_t[:, cols].astype(jnp.bfloat16)

    def gr_copy(slot):
        return remote(grad_send.at[slot - 1], grad_recv.at[slot - 1], gr_send.at[slot - 1],
                      gr_recv.at[slot - 1], x_peer if slot == 2 else core_peer, s)

    compute(0)
    for hop in (2, 3, 4):
        kv_arrived(2, hop)
        kv_head(3, hop).start()
    for hop in range(HOPS):
        kv_arrived(3, hop)
    compute(3)
    gr_copy(3).start()
    compute(2)
    gr_copy(3).wait_recv()
    grad_send[1] = (grad_send[1].astype(jnp.float32)
                    + grad_recv[2].astype(jnp.float32)).astype(jnp.bfloat16)
    gr_copy(2).start()
    for hop in range(HOPS):
        kv_arrived(1, hop)
    compute(1)
    gr_copy(1).start()
    gr_copy(1).wait_recv()
    gr_copy(2).wait_recv()

    def total(hop):
        return (grad_own[hop] + grad_recv[0, hop].astype(jnp.float32)
                + grad_recv[1, hop].astype(jnp.float32))

    def sq_copy(hop):
        return remote(seq_send.at[hop - 1], seq_recv.at[hop - 1], sq_send.at[hop - 1],
                      sq_recv.at[hop - 1], m, s - (hop if hop <= 2 else 2))

    for hop in (4, 3):
        @pl.when(s >= hop)
        def _(hop=hop):
            seq_send[hop - 1] = total(hop).astype(jnp.bfloat16)
            sq_copy(hop).start()
    for hop in (2, 1):
        grad_own[hop] = total(hop)

        @pl.when((s >= hop) & (s < seq_count - 2))
        def _(hop=hop):
            sq_copy(hop + 2).wait_recv()
            grad_own[hop] = grad_own[hop] + seq_recv[hop + 1].astype(jnp.float32)

        @pl.when(s >= hop)
        def _(hop=hop):
            seq_send[hop - 1] = grad_own[hop].astype(jnp.bfloat16)
            sq_copy(hop).start()
    grad_own[0] = total(0)
    for hop in (2, 1):
        @pl.when(s < seq_count - hop)
        def _(hop=hop):
            sq_copy(hop).wait_recv()
            grad_own[0] = grad_own[0] + seq_recv[hop - 1].astype(jnp.float32)
    dk_ref[...] = grad_own[0, 0:DH, :].T
    dv_ref[...] = grad_own[0, DH:, :].T

    for slot in (0, 1, 2, 3):
        store(slot, 0).wait()
        store(slot, 1).wait()
    for hop in (1, 2):
        @pl.when(s < seq_count - hop)
        def _(hop=hop):
            kv_seq(0, hop).wait_send()

        @pl.when((s >= hop) & (s < seq_count - 2))
        def _(hop=hop):
            kv_seq(hop, hop + 2).wait_send()
    for slot in (1, 2, 3):
        for hop in range(HOPS):
            kv_head(slot, hop).wait_send()
        gr_copy(slot).wait_send()
    for hop in range(1, HOPS):
        @pl.when(s >= hop)
        def _(hop=hop):
            sq_copy(hop).wait_send()


def shards(queries, trunk_keys, trunk_values, out_grad, segment_ids):
    rows = trunk_keys.shape[0]
    width = queries.shape[2]
    heads = lax.axis_size("head")
    seq_count = lax.axis_size("seq")
    group_size = width // (DH * heads)
    slab = group_size * DH
    vmem = pl.BlockSpec(memory_space=pltpu.VMEM)
    hbm = pl.BlockSpec(memory_space=pl.ANY)
    bf16, f32 = jnp.bfloat16, jnp.float32
    dma = pltpu.SemaphoreType.DMA
    big = jax.ShapeDtypeStruct(queries.shape, bf16)
    small = jax.ShapeDtypeStruct(trunk_keys.shape, f32)
    return tuple(pl.pallas_call(
        functools.partial(kernel, seq_count, heads, group_size),
        out_shape=(big, big, small, small),
        in_specs=[hbm, vmem, vmem, hbm, vmem],
        out_specs=(hbm, hbm, vmem, vmem),
        scratch_shapes=[
            pltpu.VMEM((heads, HOPS, 2 * rows + 16, DH), bf16),
            pltpu.VMEM((heads, rows, slab), bf16),
            pltpu.VMEM((heads, rows, slab), bf16),
            pltpu.VMEM((heads, rows, slab), bf16),
            pltpu.VMEM((heads, rows, slab), bf16),
            pltpu.VMEM((HOPS * rows, DH), bf16),
            pltpu.VMEM((HOPS * rows, DH), bf16),
            pltpu.VMEM((rows, SPAN * rows), f32),
            pltpu.VMEM((group_size * rows, HOPS * rows), bf16),
            pltpu.VMEM((group_size * rows, HOPS * rows), bf16),
            pltpu.VMEM((HOPS, 2 * DH, rows), f32),
            pltpu.VMEM((3, HOPS, 2 * DH, rows), bf16),
            pltpu.VMEM((3, HOPS, 2 * DH, rows), bf16),
            pltpu.VMEM((SPAN, 2 * DH, rows), bf16),
            pltpu.VMEM((SPAN, 2 * DH, rows), bf16),
            dma((2, heads)), dma((2, heads)),
            dma((heads, HOPS)), dma((HOPS,)), dma((heads, HOPS)),
            dma((3,)), dma((3,)), dma((SPAN,)), dma((SPAN,)),
        ],
        compiler_params=pltpu.CompilerParams(
            collective_id=0, has_side_effects=True, vmem_limit_bytes=40 * 1024 * 1024),
        cost_estimate=pl.CostEstimate(
            flops=12 * rows * rows * HOPS * width, bytes_accessed=8 * rows * width,
            transcendentals=rows * rows * HOPS * width // DH),
    )(queries, trunk_keys, trunk_values, out_grad, segment_ids.reshape(1, rows)))


def solution(mesh):
    placed = (
        P("head", "seq", None),
        P("seq", "head"),
        P("seq", "head"),
        P("head", "seq", None),
        P("seq"),
    )
    return jax.shard_map(
        shards,
        mesh=mesh,
        in_specs=placed,
        out_specs=(
            P("head", "seq", None),
            P("head", "seq", None),
            P("seq", "head"),
            P("seq", "head"),
        ),
        check_vma=False,
    )
```

```python
import functools
import math

import jax
import jax.numpy as jnp
from jax import lax
from jax.experimental import pallas as pl
from jax.experimental.pallas import tpu as pltpu
from jax.sharding import PartitionSpec as P

DH = 128
SPAN = 4
HOPS = SPAN + 1
BLOCK_ORDER = (1, 2, 3, 0, 4)
MESH = pl.DeviceIdType.MESH
NT = (((1,), (1,)), ((), ()))
NN = (((1,), (0,)), ((), ()))
TN = (((0,), (0,)), ((), ()))


def dot(a, b, dims):
    return lax.dot_general(a, b, dims, preferred_element_type=jnp.float32)


def kernel(
    seq_count, heads, group_size,
    q_hbm, k_ref, v_ref, g_hbm, seg_ref,
    out_hbm, dq_hbm, dk_ref, dv_ref,
    kv, qbuf, gbuf, obuf, dqbuf, kc, vc, bias, pscr, dscr,
    grad_own, grad_send, grad_recv, seq_send, seq_recv,
    in_sem, out_sem, kv_recv, kv_seq_send, kv_head_send,
    gr_send, gr_recv, sq_send, sq_recv,
):
    m = lax.axis_index("head")
    s = lax.axis_index("seq")
    rows = k_ref.shape[0]
    slab = group_size * DH
    scaling = 1.0 / math.sqrt(DH)
    core_peer = m + 1 - 2 * (m % 2)
    x_peer = (m + 2) % heads
    both_peer = (core_peer + 2) % heads
    groups = (m, core_peer, x_peer, both_peer)

    def columns(slot):
        return pl.ds(pl.multiple_of(groups[slot] * slab, DH), slab)

    def load(slot, which):
        src, dst = ((q_hbm, qbuf), (g_hbm, gbuf))[which]
        return pltpu.make_async_copy(
            src.at[0, :, columns(slot)], dst.at[slot], in_sem.at[which, slot])

    def store(slot, which):
        src, dst = ((obuf, out_hbm), (dqbuf, dq_hbm))[which]
        return pltpu.make_async_copy(
            src.at[slot], dst.at[0, :, columns(slot)], out_sem.at[which, slot])

    def remote(src, dst, send, recv, head, seq):
        return pltpu.make_async_remote_copy(
            src_ref=src, dst_ref=dst, send_sem=send, recv_sem=recv,
            device_id=(head, seq), device_id_type=MESH)

    def kv_seq(src_hop, dst_hop):
        return remote(kv.at[0, src_hop], kv.at[0, dst_hop], kv_seq_send.at[dst_hop],
                      kv_recv.at[0, dst_hop], m, s + (dst_hop - src_hop))

    def kv_head(slot, hop):
        src = kv.at[2 if slot == 3 else 0, hop]
        return remote(src, kv.at[slot, hop], kv_head_send.at[slot, hop],
                      kv_recv.at[slot, hop], x_peer if slot == 2 else core_peer, s)

    def kv_arrived(slot, hop):
        kv_head(slot, hop).wait_recv()

    for slot in (0, 1, 2, 3):
        load(slot, 0).start()
        load(slot, 1).start()

    kv[0, 0, 0:rows, :] = k_ref[...]
    kv[0, 0, rows:2 * rows, :] = v_ref[...]
    kv[0, 0, 2 * rows:, :] = jnp.broadcast_to(
        seg_ref[...].astype(jnp.float32), (16, rows)).astype(jnp.bfloat16)

    barrier = pltpu.get_barrier_semaphore()
    for peer in (core_peer, x_peer):
        pl.semaphore_signal(barrier, inc=1, device_id=(peer, s), device_id_type=MESH)
    expected = 2
    for step in (-2, -1, 1, 2):
        valid = (s >= -step) if step < 0 else (s < seq_count - step)

        @pl.when(valid)
        def _(step=step):
            pl.semaphore_signal(barrier, inc=1, device_id=(m, s + step), device_id_type=MESH)
        expected = expected + jnp.where(valid, 1, 0)
    pl.semaphore_wait(barrier, expected)

    for hop in (1, 2):
        @pl.when(s < seq_count - hop)
        def _(hop=hop):
            kv_seq(0, hop).start()
    kv_head(2, 0).start()
    kv_head(1, 0).start()

    for hop in range(1, HOPS):
        src_hop = hop if hop <= 2 else hop - 2

        @pl.when(s < hop)
        def _(hop=hop):
            kv[0, hop, 0:2 * rows, :] = jnp.zeros((2 * rows, DH), jnp.bfloat16)
            kv[0, hop, 2 * rows:, :] = jnp.full((16, DH), -1.0, jnp.bfloat16)

        @pl.when(s >= hop)
        def _(hop=hop):
            kv_seq(0 if hop <= 2 else hop - 2, hop).wait_recv()

        if hop <= 2:
            @pl.when((s >= hop) & (s < seq_count - 2))
            def _(hop=hop):
                kv_seq(hop, hop + 2).start()
        kv_head(2, hop).start()
        kv_head(1, hop).start()
        if hop >= 3:
            kv_arrived(2, hop - 3)
            kv_head(3, hop - 3).start()

    row_id = lax.broadcasted_iota(jnp.int32, (rows, rows), 0)
    col_id = lax.broadcasted_iota(jnp.int32, (rows, rows), 1)
    tri = col_id <= row_id

    def seg_row(hop):
        full = kv[0, hop, 2 * rows:, :].astype(jnp.float32)
        return full[0:1, :]

    seg_q = jnp.sum(jnp.where(row_id == col_id, seg_row(0), 0.0), axis=1, keepdims=True)
    for at, hop in enumerate((1, 2, 3)):
        bias[:, at * rows:(at + 1) * rows] = jnp.where(seg_row(hop) == seg_q, 0.0, -1e30)
    bias[:, 3 * rows:] = jnp.where(
        jnp.where(tri, seg_row(0), seg_row(4)) == seg_q, 0.0, -1e30)

    shared = 3 * rows

    def fold(x):
        edge = jnp.where(tri, x[:, shared:shared + rows], x[:, shared + rows:])
        return jnp.concatenate([x[:, :shared], edge], axis=1)

    def unfold(x):
        edge = x[:, shared:]
        zero = jnp.zeros_like(edge)
        return jnp.concatenate(
            [x[:, :shared], jnp.where(tri, edge, zero), jnp.where(tri, zero, edge)],
            axis=1).astype(jnp.bfloat16)

    def compute(slot):
        load(slot, 0).wait()
        load(slot, 1).wait()
        for at, hop in enumerate(BLOCK_ORDER):
            kc[at * rows:(at + 1) * rows, :] = kv[slot, hop, 0:rows, :]
            vc[at * rows:(at + 1) * rows, :] = kv[slot, hop, rows:2 * rows, :]

        q_rows = jnp.concatenate(
            [qbuf[slot, :, r * DH:(r + 1) * DH] for r in range(group_size)], axis=0)
        g_rows = jnp.concatenate(
            [gbuf[slot, :, r * DH:(r + 1) * DH] for r in range(group_size)], axis=0)
        raw = dot(q_rows, kc[...], NT)
        dprobs = dot(g_rows, vc[...], NT)
        for r in range(group_size):
            here = slice(r * rows, (r + 1) * rows)
            t = fold(raw[here]) * (scaling * math.log2(math.e)) + bias[...]
            e = jnp.exp2(t - jnp.max(t, axis=1, keepdims=True))
            probs = e * (1.0 / jnp.sum(e, axis=1, keepdims=True))
            pscr[here, :] = unfold(probs)
            weighted = probs * fold(dprobs[here])
            delta = jnp.sum(weighted, axis=1, keepdims=True)
            dscr[here, :] = unfold(weighted - probs * delta)
        out32 = dot(pscr[...], vc[...], NN)
        dq32 = dot(dscr[...], kc[...], NN) * scaling
        for r in range(group_size):
            here = slice(r * rows, (r + 1) * rows)
            cols = slice(r * DH, (r + 1) * DH)
            obuf[slot, :, cols] = out32[here].astype(jnp.bfloat16)
            dqbuf[slot, :, cols] = dq32[here].astype(jnp.bfloat16)
        store(slot, 0).start()
        store(slot, 1).start()
        key_t = dot(q_rows, dscr[...], TN) * scaling
        value_t = dot(g_rows, pscr[...], TN)
        for at, hop in enumerate(BLOCK_ORDER):
            cols = slice(at * rows, (at + 1) * rows)
            if slot == 0:
                grad_own[hop, 0:DH, :] = key_t[:, cols]
                grad_own[hop, DH:, :] = value_t[:, cols]
            else:
                grad_send[slot - 1, hop, 0:DH, :] = key_t[:, cols].astype(jnp.bfloat16)
                grad_send[slot - 1, hop, DH:, :] = value_t[:, cols].astype(jnp.bfloat16)

    def gr_copy(slot):
        return remote(grad_send.at[slot - 1], grad_recv.at[slot - 1], gr_send.at[slot - 1],
                      gr_recv.at[slot - 1], x_peer if slot == 2 else core_peer, s)

    compute(0)
    for hop in (2, 3, 4):
        kv_arrived(2, hop)
        kv_head(3, hop).start()
    for hop in range(HOPS):
        kv_arrived(3, hop)
    compute(3)
    gr_copy(3).start()
    compute(2)
    gr_copy(3).wait_recv()
    grad_send[1] = (grad_send[1].astype(jnp.float32)
                    + grad_recv[2].astype(jnp.float32)).astype(jnp.bfloat16)
    gr_copy(2).start()
    for hop in range(HOPS):
        kv_arrived(1, hop)
    compute(1)
    gr_copy(1).start()
    gr_copy(1).wait_recv()
    gr_copy(2).wait_recv()

    def total(hop):
        return (grad_own[hop] + grad_recv[0, hop].astype(jnp.float32)
                + grad_recv[1, hop].astype(jnp.float32))

    def sq_copy(hop):
        return remote(seq_send.at[hop - 1], seq_recv.at[hop - 1], sq_send.at[hop - 1],
                      sq_recv.at[hop - 1], m, s - (hop if hop <= 2 else 2))

    for hop in (4, 3):
        @pl.when(s >= hop)
        def _(hop=hop):
            seq_send[hop - 1] = total(hop).astype(jnp.bfloat16)
            sq_copy(hop).start()
    for hop in (2, 1):
        grad_own[hop] = total(hop)

        @pl.when((s >= hop) & (s < seq_count - 2))
        def _(hop=hop):
            sq_copy(hop + 2).wait_recv()
            grad_own[hop] = grad_own[hop] + seq_recv[hop + 1].astype(jnp.float32)

        @pl.when(s >= hop)
        def _(hop=hop):
            seq_send[hop - 1] = grad_own[hop].astype(jnp.bfloat16)
            sq_copy(hop).start()
    grad_own[0] = total(0)
    for hop in (2, 1):
        @pl.when(s < seq_count - hop)
        def _(hop=hop):
            sq_copy(hop).wait_recv()
            grad_own[0] = grad_own[0] + seq_recv[hop - 1].astype(jnp.float32)
    dk_ref[...] = grad_own[0, 0:DH, :].T
    dv_ref[...] = grad_own[0, DH:, :].T

    for slot in (0, 1, 2, 3):
        store(slot, 0).wait()
        store(slot, 1).wait()
    for hop in (1, 2):
        @pl.when(s < seq_count - hop)
        def _(hop=hop):
            kv_seq(0, hop).wait_send()

        @pl.when((s >= hop) & (s < seq_count - 2))
        def _(hop=hop):
            kv_seq(hop, hop + 2).wait_send()
    for slot in (1, 2, 3):
        for hop in range(HOPS):
            kv_head(slot, hop).wait_send()
        gr_copy(slot).wait_send()
    for hop in range(1, HOPS):
        @pl.when(s >= hop)
        def _(hop=hop):
            sq_copy(hop).wait_send()


def shards(queries, trunk_keys, trunk_values, out_grad, segment_ids):
    rows = trunk_keys.shape[0]
    width = queries.shape[2]
    heads = lax.axis_size("head")
    seq_count = lax.axis_size("seq")
    group_size = width // (DH * heads)
    slab = group_size * DH
    vmem = pl.BlockSpec(memory_space=pltpu.VMEM)
    hbm = pl.BlockSpec(memory_space=pl.ANY)
    bf16, f32 = jnp.bfloat16, jnp.float32
    dma = pltpu.SemaphoreType.DMA
    big = jax.ShapeDtypeStruct(queries.shape, bf16)
    small = jax.ShapeDtypeStruct(trunk_keys.shape, f32)
    return tuple(pl.pallas_call(
        functools.partial(kernel, seq_count, heads, group_size),
        out_shape=(big, big, small, small),
        in_specs=[hbm, vmem, vmem, hbm, vmem],
        out_specs=(hbm, hbm, vmem, vmem),
        scratch_shapes=[
            pltpu.VMEM((heads, HOPS, 2 * rows + 16, DH), bf16),
            pltpu.VMEM((heads, rows, slab), bf16),
            pltpu.VMEM((heads, rows, slab), bf16),
            pltpu.VMEM((heads, rows, slab), bf16),
            pltpu.VMEM((heads, rows, slab), bf16),
            pltpu.VMEM((HOPS * rows, DH), bf16),
            pltpu.VMEM((HOPS * rows, DH), bf16),
            pltpu.VMEM((rows, SPAN * rows), f32),
            pltpu.VMEM((group_size * rows, HOPS * rows), bf16),
            pltpu.VMEM((group_size * rows, HOPS * rows), bf16),
            pltpu.VMEM((HOPS, 2 * DH, rows), f32),
            pltpu.VMEM((3, HOPS, 2 * DH, rows), bf16),
            pltpu.VMEM((3, HOPS, 2 * DH, rows), bf16),
            pltpu.VMEM((SPAN, 2 * DH, rows), bf16),
            pltpu.VMEM((SPAN, 2 * DH, rows), bf16),
            dma((2, heads)), dma((2, heads)),
            dma((heads, HOPS)), dma((HOPS,)), dma((heads, HOPS)),
            dma((3,)), dma((3,)), dma((SPAN,)), dma((SPAN,)),
        ],
        compiler_params=pltpu.CompilerParams(
            collective_id=0, has_side_effects=True, vmem_limit_bytes=62 * 1024 * 1024),
        cost_estimate=pl.CostEstimate(
            flops=12 * rows * rows * HOPS * width, bytes_accessed=8 * rows * width,
            transcendentals=rows * rows * HOPS * width // DH),
    )(queries, trunk_keys, trunk_values, out_grad, segment_ids.reshape(1, rows)))


def solution(mesh):
    placed = (
        P("head", "seq", None),
        P("seq", "head"),
        P("seq", "head"),
        P("head", "seq", None),
        P("seq"),
    )
    return jax.shard_map(
        shards,
        mesh=mesh,
        in_specs=placed,
        out_specs=(
            P("head", "seq", None),
            P("head", "seq", None),
            P("seq", "head"),
            P("seq", "head"),
        ),
        check_vma=False,
    )
```

```python
import functools
import math

import jax
import jax.numpy as jnp
from jax import lax
from jax.experimental import pallas as pl
from jax.experimental.pallas import tpu as pltpu
from jax.sharding import PartitionSpec as P

DH = 128
SPAN = 4
HOPS = SPAN + 1
BLOCK_ORDER = (1, 2, 3, 0, 4)
PARTS = ((3, 2), (1, 2), (0, 1))
PIECES = 1
MESH = pl.DeviceIdType.MESH
NT = (((1,), (1,)), ((), ()))
NN = (((1,), (0,)), ((), ()))
TN = (((0,), (0,)), ((), ()))


def dot(a, b, dims):
    return lax.dot_general(a, b, dims, preferred_element_type=jnp.float32)


def kernel(
    seq_count, heads, group_size,
    q_hbm, k_hbm, v_hbm, g_hbm, seg_hbm,
    out_hbm, dq_hbm, dk_ref, dv_ref,
    seg, kv, qbuf, gbuf, obuf, dqbuf, kc, vc, bias, pscr, dscr,
    grad_own, grad_send, grad_recv, seq_send, seq_recv,
    own_sem, in_sem, out_sem, kv_recv, kv_seq_send, kv_head_send,
    gr_send, gr_recv, sq_send, sq_recv,
):
    m = lax.axis_index("head")
    s = lax.axis_index("seq")
    rows = k_hbm.shape[0]
    slab = group_size * DH
    scaling = 1.0 / math.sqrt(DH)
    core_peer = m + 1 - 2 * (m % 2)
    x_peer = (m + 2) % heads
    both_peer = (core_peer + 2) % heads
    groups = (m, core_peer, x_peer, both_peer)

    def columns(slot):
        return pl.ds(pl.multiple_of(groups[slot] * slab, DH), slab)

    def load(slot, which):
        src, dst = ((q_hbm, qbuf), (g_hbm, gbuf))[which]
        return pltpu.make_async_copy(
            src.at[0, :, columns(slot)], dst.at[slot], in_sem.at[which, slot])

    def store(slot, which):
        src, dst = ((obuf, out_hbm), (dqbuf, dq_hbm))[which]
        return pltpu.make_async_copy(
            src.at[slot], dst.at[0, :, columns(slot)], out_sem.at[which, slot])

    def remote(src, dst, send, recv, head, seq):
        return pltpu.make_async_remote_copy(
            src_ref=src, dst_ref=dst, send_sem=send, recv_sem=recv,
            device_id=(head, seq), device_id_type=MESH)

    def kv_seq(src_hop, dst_hop):
        return remote(kv.at[0, src_hop], kv.at[0, dst_hop], kv_seq_send.at[dst_hop],
                      kv_recv.at[0, dst_hop], m, s + (dst_hop - src_hop))

    def kv_head(slot, hop):
        src = kv.at[2 if slot == 3 else 0, hop]
        return remote(src, kv.at[slot, hop], kv_head_send.at[slot, hop],
                      kv_recv.at[slot, hop], x_peer if slot == 2 else core_peer, s)

    def kv_arrived(slot, hop):
        kv_head(slot, hop).wait_recv()

    own = (
        pltpu.make_async_copy(k_hbm, kv.at[0, 0, 0:rows, :], own_sem.at[0]),
        pltpu.make_async_copy(v_hbm, kv.at[0, 0, rows:2 * rows, :], own_sem.at[1]),
        pltpu.make_async_copy(seg_hbm, seg, own_sem.at[2]),
    )
    for copy in own:
        copy.start()

    barrier = pltpu.get_barrier_semaphore()
    for peer in (core_peer, x_peer):
        pl.semaphore_signal(barrier, inc=1, device_id=(peer, s), device_id_type=MESH)
    expected = 2
    for step in (-2, -1, 1, 2):
        valid = (s >= -step) if step < 0 else (s < seq_count - step)

        @pl.when(valid)
        def _(step=step):
            pl.semaphore_signal(barrier, inc=1, device_id=(m, s + step), device_id_type=MESH)
        expected = expected + jnp.where(valid, 1, 0)

    for copy in own:
        copy.wait()
    for slot in (0, 1, 2, 3):
        load(slot, 0).start()
        load(slot, 1).start()
    kv[0, 0, 2 * rows:, :] = jnp.broadcast_to(
        seg[...].astype(jnp.float32), (16, rows)).astype(jnp.bfloat16)
    pl.semaphore_wait(barrier, expected)

    for hop in (1, 2):
        @pl.when(s < seq_count - hop)
        def _(hop=hop):
            kv_seq(0, hop).start()
    kv_head(2, 0).start()
    kv_head(1, 0).start()

    for hop in range(1, HOPS):
        src_hop = hop if hop <= 2 else hop - 2

        @pl.when(s < hop)
        def _(hop=hop):
            kv[0, hop, 0:2 * rows, :] = jnp.zeros((2 * rows, DH), jnp.bfloat16)
            kv[0, hop, 2 * rows:, :] = jnp.full((16, DH), -1.0, jnp.bfloat16)

        @pl.when(s >= hop)
        def _(hop=hop):
            kv_seq(0 if hop <= 2 else hop - 2, hop).wait_recv()

        if hop <= 2:
            @pl.when((s >= hop) & (s < seq_count - 2))
            def _(hop=hop):
                kv_seq(hop, hop + 2).start()
        kv_head(2, hop).start()
        kv_head(1, hop).start()
        if hop >= 3:
            kv_arrived(2, hop - 3)
            kv_head(3, hop - 3).start()

    row_id = lax.broadcasted_iota(jnp.int32, (rows, rows), 0)
    col_id = lax.broadcasted_iota(jnp.int32, (rows, rows), 1)
    tri = col_id <= row_id

    def seg_row(hop):
        full = kv[0, hop, 2 * rows:, :].astype(jnp.float32)
        return full[0:1, :]

    seg_q = jnp.sum(jnp.where(row_id == col_id, seg_row(0), 0.0), axis=1, keepdims=True)
    for at, hop in enumerate((1, 2, 3)):
        bias[:, at * rows:(at + 1) * rows] = jnp.where(seg_row(hop) == seg_q, 0.0, -1e30)
    bias[:, 3 * rows:] = jnp.where(
        jnp.where(tri, seg_row(0), seg_row(4)) == seg_q, 0.0, -1e30)

    shared = 3 * rows

    def fold(x):
        edge = jnp.where(tri, x[:, shared:shared + rows], x[:, shared + rows:])
        return jnp.concatenate([x[:, :shared], edge], axis=1)

    def unfold(x):
        edge = x[:, shared:]
        zero = jnp.zeros_like(edge)
        return jnp.concatenate(
            [x[:, :shared], jnp.where(tri, edge, zero), jnp.where(tri, zero, edge)],
            axis=1).astype(jnp.bfloat16)

    def compute(slot):
        load(slot, 0).wait()
        load(slot, 1).wait()
        for at, hop in enumerate(BLOCK_ORDER):
            kc[at * rows:(at + 1) * rows, :] = kv[slot, hop, 0:rows, :]
            vc[at * rows:(at + 1) * rows, :] = kv[slot, hop, rows:2 * rows, :]

        q_rows = jnp.concatenate(
            [qbuf[slot, :, r * DH:(r + 1) * DH] for r in range(group_size)], axis=0)
        g_rows = jnp.concatenate(
            [gbuf[slot, :, r * DH:(r + 1) * DH] for r in range(group_size)], axis=0)
        raw = dot(q_rows, kc[...], NT)
        dprobs = dot(g_rows, vc[...], NT)
        for r in range(group_size):
            here = slice(r * rows, (r + 1) * rows)
            t = fold(raw[here]) * (scaling * math.log2(math.e)) + bias[...]
            e = jnp.exp2(t - jnp.max(t, axis=1, keepdims=True))
            probs = e * (1.0 / jnp.sum(e, axis=1, keepdims=True))
            pscr[here, :] = unfold(probs)
            weighted = probs * fold(dprobs[here])
            delta = jnp.sum(weighted, axis=1, keepdims=True)
            dscr[here, :] = unfold(weighted - probs * delta)
        out32 = dot(pscr[...], vc[...], NN)
        dq32 = dot(dscr[...], kc[...], NN) * scaling
        for r in range(group_size):
            here = slice(r * rows, (r + 1) * rows)
            cols = slice(r * DH, (r + 1) * DH)
            obuf[slot, :, cols] = out32[here].astype(jnp.bfloat16)
            dqbuf[slot, :, cols] = dq32[here].astype(jnp.bfloat16)
        store(slot, 0).start()
        store(slot, 1).start()
        key_t = dot(q_rows, dscr[...], TN) * scaling
        value_t = dot(g_rows, pscr[...], TN)
        for at, hop in enumerate(BLOCK_ORDER):
            cols = slice(at * rows, (at + 1) * rows)
            if slot == 0:
                grad_own[hop, 0:DH, :] = key_t[:, cols]
                grad_own[hop, DH:, :] = value_t[:, cols]
            else:
                grad_send[slot - 1, hop, 0:DH, :] = key_t[:, cols].astype(jnp.bfloat16)
                grad_send[slot - 1, hop, DH:, :] = value_t[:, cols].astype(jnp.bfloat16)

    def gr_copy(slot, part):
        hops = pl.ds(*PARTS[part])
        return remote(grad_send.at[slot - 1, hops], grad_recv.at[slot - 1, hops],
                      gr_send.at[slot - 1, part], gr_recv.at[slot - 1, part],
                      x_peer if slot == 2 else core_peer, s)

    compute(0)
    for hop in (2, 3, 4):
        kv_arrived(2, hop)
        kv_head(3, hop).start()
    for hop in range(HOPS):
        kv_arrived(1, hop)
    compute(1)
    for part in range(len(PARTS)):
        gr_copy(1, part).start()
    compute(2)
    for hop in range(HOPS):
        kv_arrived(3, hop)
    compute(3)
    for part in range(len(PARTS)):
        gr_copy(3, part).start()
    for part, (first, count) in enumerate(PARTS):
        hops = slice(first, first + count)
        gr_copy(3, part).wait_recv()
        grad_send[1, hops] = (grad_send[1, hops].astype(jnp.float32)
                              + grad_recv[2, hops].astype(jnp.float32)).astype(jnp.bfloat16)
        gr_copy(2, part).start()

    def gr_arrived(part):
        gr_copy(1, part).wait_recv()
        gr_copy(2, part).wait_recv()

    def total(hop):
        return (grad_own[hop] + grad_recv[0, hop].astype(jnp.float32)
                + grad_recv[1, hop].astype(jnp.float32))

    def sq_copy(hop):
        return remote(seq_send.at[hop - 1], seq_recv.at[hop - 1], sq_send.at[hop - 1],
                      sq_recv.at[hop - 1], m, s - (hop if hop <= 2 else 2))

    gr_arrived(0)
    for hop in (4, 3):
        @pl.when(s >= hop)
        def _(hop=hop):
            seq_send[hop - 1] = total(hop).astype(jnp.bfloat16)
            sq_copy(hop).start()
    gr_arrived(1)
    for hop in (2, 1):
        grad_own[hop] = total(hop)

        @pl.when((s >= hop) & (s < seq_count - 2))
        def _(hop=hop):
            sq_copy(hop + 2).wait_recv()
            grad_own[hop] = grad_own[hop] + seq_recv[hop + 1].astype(jnp.float32)

        @pl.when(s >= hop)
        def _(hop=hop):
            seq_send[hop - 1] = grad_own[hop].astype(jnp.bfloat16)
            sq_copy(hop).start()
    gr_arrived(2)
    grad_own[0] = total(0)
    for hop in (2, 1):
        @pl.when(s < seq_count - hop)
        def _(hop=hop):
            sq_copy(hop).wait_recv()
            grad_own[0] = grad_own[0] + seq_recv[hop - 1].astype(jnp.float32)
    dk_ref[...] = grad_own[0, 0:DH, :].T
    dv_ref[...] = grad_own[0, DH:, :].T

    for slot in (0, 1, 2, 3):
        store(slot, 0).wait()
        store(slot, 1).wait()
    for hop in (1, 2):
        @pl.when(s < seq_count - hop)
        def _(hop=hop):
            kv_seq(0, hop).wait_send()

        @pl.when((s >= hop) & (s < seq_count - 2))
        def _(hop=hop):
            kv_seq(hop, hop + 2).wait_send()
    for slot in (1, 2, 3):
        for hop in range(HOPS):
            kv_head(slot, hop).wait_send()
        for part in range(len(PARTS)):
            gr_copy(slot, part).wait_send()
    for hop in range(1, HOPS):
        @pl.when(s >= hop)
        def _(hop=hop):
            sq_copy(hop).wait_send()


def hand_over(a, b, c, d, a_out, b_out, c_out, d_out, a_on, b_on, c_on, d_on, in_sem, out_sem):
    loads, stores = [], []
    for at, (src, on, dst) in enumerate(
            ((a, a_on, a_out), (b, b_on, b_out), (c, c_on, c_out), (d, d_on, d_out))):
        pieces = PIECES if len(src.shape) == 3 else 1
        size = src.shape[-2] // pieces
        for n in range(pieces):
            part = pl.ds(n * size, size)
            part = (0, part) if len(src.shape) == 3 else (part,)
            loads.append(pltpu.make_async_copy(src.at[part], on.at[part], in_sem.at[at, n]))
            stores.append(pltpu.make_async_copy(on.at[part], dst.at[part], out_sem.at[at, n]))
    for load in loads:
        load.start()
    for load, store in zip(loads, stores):
        load.wait()
        store.start()
    for store in stores:
        store.wait()


def shards(queries, trunk_keys, trunk_values, out_grad, segment_ids):
    rows = trunk_keys.shape[0]
    width = queries.shape[2]
    heads = lax.axis_size("head")
    seq_count = lax.axis_size("seq")
    group_size = width // (DH * heads)
    slab = group_size * DH
    vmem = pl.BlockSpec(memory_space=pltpu.VMEM)
    hbm = pl.BlockSpec(memory_space=pltpu.HBM)
    free = pl.BlockSpec(memory_space=pl.ANY)
    bf16, f32 = jnp.bfloat16, jnp.float32
    dma = pltpu.SemaphoreType.DMA
    big = jax.ShapeDtypeStruct(queries.shape, bf16)
    small = jax.ShapeDtypeStruct(trunk_keys.shape, f32)
    results = pl.pallas_call(
        functools.partial(kernel, seq_count, heads, group_size),
        out_shape=(big, big, small, small),
        in_specs=[hbm] * 5,
        out_specs=(free, free, vmem, vmem),
        scratch_shapes=[
            pltpu.VMEM((1, rows), jnp.int32),
            pltpu.VMEM((heads, HOPS, 2 * rows + 16, DH), bf16),
            pltpu.VMEM((heads, rows, slab), bf16),
            pltpu.VMEM((heads, rows, slab), bf16),
            pltpu.VMEM((heads, rows, slab), bf16),
            pltpu.VMEM((heads, rows, slab), bf16),
            pltpu.VMEM((HOPS * rows, DH), bf16),
            pltpu.VMEM((HOPS * rows, DH), bf16),
            pltpu.VMEM((rows, SPAN * rows), f32),
            pltpu.VMEM((group_size * rows, HOPS * rows), bf16),
            pltpu.VMEM((group_size * rows, HOPS * rows), bf16),
            pltpu.VMEM((HOPS, 2 * DH, rows), f32),
            pltpu.VMEM((3, HOPS, 2 * DH, rows), bf16),
            pltpu.VMEM((3, HOPS, 2 * DH, rows), bf16),
            pltpu.VMEM((SPAN, 2 * DH, rows), bf16),
            pltpu.VMEM((SPAN, 2 * DH, rows), bf16),
            dma((3,)), dma((2, heads)), dma((2, heads)),
            dma((heads, HOPS)), dma((HOPS,)), dma((heads, HOPS)),
            dma((3, len(PARTS))), dma((3, len(PARTS))), dma((SPAN,)), dma((SPAN,)),
        ],
        compiler_params=pltpu.CompilerParams(
            collective_id=0, has_side_effects=True, vmem_limit_bytes=62 * 1024 * 1024),
        cost_estimate=pl.CostEstimate(
            flops=12 * rows * rows * HOPS * width, bytes_accessed=8 * rows * width,
            transcendentals=rows * rows * HOPS * width // DH),
    )(queries, trunk_keys, trunk_values, out_grad, segment_ids.reshape(1, rows))
    return tuple(pl.pallas_call(
        hand_over,
        out_shape=(big, big, small, small),
        in_specs=[free] * 4,
        out_specs=(free,) * 4,
        scratch_shapes=[
            pltpu.VMEM(big.shape, bf16), pltpu.VMEM(big.shape, bf16),
            pltpu.VMEM(small.shape, f32), pltpu.VMEM(small.shape, f32),
            dma((4, PIECES)), dma((4, PIECES)),
        ],
        compiler_params=pltpu.CompilerParams(vmem_limit_bytes=62 * 1024 * 1024),
    )(*results))


def solution(mesh):
    placed = (
        P("head", "seq", None),
        P("seq", "head"),
        P("seq", "head"),
        P("head", "seq", None),
        P("seq"),
    )
    return jax.shard_map(
        shards,
        mesh=mesh,
        in_specs=placed,
        out_specs=(
            P("head", "seq", None),
            P("head", "seq", None),
            P("seq", "head"),
            P("seq", "head"),
        ),
        check_vma=False,
    )
```

```python
import functools
import math

import jax
import jax.numpy as jnp
from jax import lax
from jax.experimental import pallas as pl
from jax.experimental.pallas import tpu as pltpu
from jax.sharding import PartitionSpec as P

DH = 128
SPAN = 4
HOPS = SPAN + 1
BLOCK_ORDER = (1, 2, 3, 0, 4)
PART_HOPS = (4, 3, 2, 1, 0)
PARTS = tuple((hop, 1) for hop in PART_HOPS)
PIECES = 1
MESH = pl.DeviceIdType.MESH
NT = (((1,), (1,)), ((), ()))
NN = (((1,), (0,)), ((), ()))
TN = (((0,), (0,)), ((), ()))


def dot(a, b, dims):
    return lax.dot_general(a, b, dims, preferred_element_type=jnp.float32)


def kernel(
    seq_count, heads, group_size,
    q_hbm, k_hbm, v_hbm, g_hbm, seg_hbm,
    out_hbm, dq_hbm, dk_ref, dv_ref,
    seg, kv, qbuf, gbuf, obuf, dqbuf, kc, vc, bias, pscr, dscr,
    grad_own, grad_send, grad_recv, seq_send, seq_recv,
    own_sem, in_sem, out_sem, kv_recv, kv_seq_send, kv_head_send,
    gr_send, gr_recv, sq_send, sq_recv,
):
    m = lax.axis_index("head")
    s = lax.axis_index("seq")
    rows = k_hbm.shape[0]
    slab = group_size * DH
    scaling = 1.0 / math.sqrt(DH)
    core_peer = m + 1 - 2 * (m % 2)
    x_peer = (m + 2) % heads
    both_peer = (core_peer + 2) % heads
    groups = (m, core_peer, x_peer, both_peer)

    def columns(slot):
        return pl.ds(pl.multiple_of(groups[slot] * slab, DH), slab)

    def load(slot, which):
        src, dst = ((q_hbm, qbuf), (g_hbm, gbuf))[which]
        return pltpu.make_async_copy(
            src.at[0, :, columns(slot)], dst.at[slot], in_sem.at[which, slot])

    def store(slot, which):
        src, dst = ((obuf, out_hbm), (dqbuf, dq_hbm))[which]
        return pltpu.make_async_copy(
            src.at[slot], dst.at[0, :, columns(slot)], out_sem.at[which, slot])

    def remote(src, dst, send, recv, head, seq):
        return pltpu.make_async_remote_copy(
            src_ref=src, dst_ref=dst, send_sem=send, recv_sem=recv,
            device_id=(head, seq), device_id_type=MESH)

    def kv_seq(src_hop, dst_hop):
        return remote(kv.at[0, src_hop], kv.at[0, dst_hop], kv_seq_send.at[dst_hop],
                      kv_recv.at[0, dst_hop], m, s + (dst_hop - src_hop))

    def kv_head(slot, hop):
        src = kv.at[2 if slot == 3 else 0, hop]
        return remote(src, kv.at[slot, hop], kv_head_send.at[slot, hop],
                      kv_recv.at[slot, hop], x_peer if slot == 2 else core_peer, s)

    def kv_arrived(slot, hop):
        kv_head(slot, hop).wait_recv()

    own = (
        pltpu.make_async_copy(k_hbm, kv.at[0, 0, 0:rows, :], own_sem.at[0]),
        pltpu.make_async_copy(v_hbm, kv.at[0, 0, rows:2 * rows, :], own_sem.at[1]),
        pltpu.make_async_copy(seg_hbm, seg, own_sem.at[2]),
    )
    for copy in own:
        copy.start()

    barrier = pltpu.get_barrier_semaphore()
    for peer in (core_peer, x_peer):
        pl.semaphore_signal(barrier, inc=1, device_id=(peer, s), device_id_type=MESH)
    expected = 2
    for step in (-2, -1, 1, 2):
        valid = (s >= -step) if step < 0 else (s < seq_count - step)

        @pl.when(valid)
        def _(step=step):
            pl.semaphore_signal(barrier, inc=1, device_id=(m, s + step), device_id_type=MESH)
        expected = expected + jnp.where(valid, 1, 0)

    for copy in own:
        copy.wait()
    for slot in (0, 1, 2, 3):
        load(slot, 0).start()
        load(slot, 1).start()
    kv[0, 0, 2 * rows:, :] = jnp.broadcast_to(
        seg[...].astype(jnp.float32), (16, rows)).astype(jnp.bfloat16)
    pl.semaphore_wait(barrier, expected)

    for hop in (1, 2):
        @pl.when(s < seq_count - hop)
        def _(hop=hop):
            kv_seq(0, hop).start()
    kv_head(2, 0).start()
    kv_head(1, 0).start()

    for hop in range(1, HOPS):
        src_hop = hop if hop <= 2 else hop - 2

        @pl.when(s < hop)
        def _(hop=hop):
            kv[0, hop, 0:2 * rows, :] = jnp.zeros((2 * rows, DH), jnp.bfloat16)
            kv[0, hop, 2 * rows:, :] = jnp.full((16, DH), -1.0, jnp.bfloat16)

        @pl.when(s >= hop)
        def _(hop=hop):
            kv_seq(0 if hop <= 2 else hop - 2, hop).wait_recv()

        if hop <= 2:
            @pl.when((s >= hop) & (s < seq_count - 2))
            def _(hop=hop):
                kv_seq(hop, hop + 2).start()
        kv_head(2, hop).start()
        kv_head(1, hop).start()
        if hop >= 3:
            kv_arrived(2, hop - 3)
            kv_head(3, hop - 3).start()

    row_id = lax.broadcasted_iota(jnp.int32, (rows, rows), 0)
    col_id = lax.broadcasted_iota(jnp.int32, (rows, rows), 1)
    tri = col_id <= row_id

    def seg_row(hop):
        full = kv[0, hop, 2 * rows:, :].astype(jnp.float32)
        return full[0:1, :]

    seg_q = jnp.sum(jnp.where(row_id == col_id, seg_row(0), 0.0), axis=1, keepdims=True)
    for at, hop in enumerate((1, 2, 3)):
        bias[:, at * rows:(at + 1) * rows] = jnp.where(seg_row(hop) == seg_q, 0.0, -1e30)
    bias[:, 3 * rows:] = jnp.where(
        jnp.where(tri, seg_row(0), seg_row(4)) == seg_q, 0.0, -1e30)

    shared = 3 * rows

    def fold(x):
        edge = jnp.where(tri, x[:, shared:shared + rows], x[:, shared + rows:])
        return jnp.concatenate([x[:, :shared], edge], axis=1)

    def unfold(x):
        edge = x[:, shared:]
        zero = jnp.zeros_like(edge)
        return jnp.concatenate(
            [x[:, :shared], jnp.where(tri, edge, zero), jnp.where(tri, zero, edge)],
            axis=1).astype(jnp.bfloat16)

    def compute(slot):
        load(slot, 0).wait()
        load(slot, 1).wait()
        for at, hop in enumerate(BLOCK_ORDER):
            kc[at * rows:(at + 1) * rows, :] = kv[slot, hop, 0:rows, :]
            vc[at * rows:(at + 1) * rows, :] = kv[slot, hop, rows:2 * rows, :]

        q_rows = jnp.concatenate(
            [qbuf[slot, :, r * DH:(r + 1) * DH] for r in range(group_size)], axis=0)
        g_rows = jnp.concatenate(
            [gbuf[slot, :, r * DH:(r + 1) * DH] for r in range(group_size)], axis=0)
        raw = dot(q_rows, kc[...], NT)
        dprobs = dot(g_rows, vc[...], NT)
        for r in range(group_size):
            here = slice(r * rows, (r + 1) * rows)
            t = fold(raw[here]) * (scaling * math.log2(math.e)) + bias[...]
            e = jnp.exp2(t - jnp.max(t, axis=1, keepdims=True))
            probs = e * (1.0 / jnp.sum(e, axis=1, keepdims=True))
            pscr[here, :] = unfold(probs)
            weighted = probs * fold(dprobs[here])
            delta = jnp.sum(weighted, axis=1, keepdims=True)
            dscr[here, :] = unfold(weighted - probs * delta)
        out32 = dot(pscr[...], vc[...], NN)
        dq32 = dot(dscr[...], kc[...], NN) * scaling
        for r in range(group_size):
            here = slice(r * rows, (r + 1) * rows)
            cols = slice(r * DH, (r + 1) * DH)
            obuf[slot, :, cols] = out32[here].astype(jnp.bfloat16)
            dqbuf[slot, :, cols] = dq32[here].astype(jnp.bfloat16)
        store(slot, 0).start()
        store(slot, 1).start()
        key_t = dot(q_rows, dscr[...], TN) * scaling
        value_t = dot(g_rows, pscr[...], TN)
        for at, hop in enumerate(BLOCK_ORDER):
            cols = slice(at * rows, (at + 1) * rows)
            if slot == 0:
                grad_own[hop, 0:DH, :] = key_t[:, cols]
                grad_own[hop, DH:, :] = value_t[:, cols]
            else:
                grad_send[slot - 1, hop, 0:DH, :] = key_t[:, cols].astype(jnp.bfloat16)
                grad_send[slot - 1, hop, DH:, :] = value_t[:, cols].astype(jnp.bfloat16)

    def gr_copy(slot, part):
        hops = pl.ds(*PARTS[part])
        return remote(grad_send.at[slot - 1, hops], grad_recv.at[slot - 1, hops],
                      gr_send.at[slot - 1, part], gr_recv.at[slot - 1, part],
                      x_peer if slot == 2 else core_peer, s)

    compute(0)
    for hop in (2, 3, 4):
        kv_arrived(2, hop)
        kv_head(3, hop).start()
    for hop in range(HOPS):
        kv_arrived(1, hop)
    compute(1)
    for part in range(len(PARTS)):
        gr_copy(1, part).start()
    compute(2)
    for hop in range(HOPS):
        kv_arrived(3, hop)
    compute(3)
    for part in range(len(PARTS)):
        gr_copy(3, part).start()
    for part, (first, count) in enumerate(PARTS):
        hops = slice(first, first + count)
        gr_copy(3, part).wait_recv()
        grad_send[1, hops] = (grad_send[1, hops].astype(jnp.float32)
                              + grad_recv[2, hops].astype(jnp.float32)).astype(jnp.bfloat16)
        gr_copy(2, part).start()

    def gr_arrived(part):
        gr_copy(1, part).wait_recv()
        gr_copy(2, part).wait_recv()

    def total(hop):
        return (grad_own[hop] + grad_recv[0, hop].astype(jnp.float32)
                + grad_recv[1, hop].astype(jnp.float32))

    def sq_copy(hop):
        return remote(seq_send.at[hop - 1], seq_recv.at[hop - 1], sq_send.at[hop - 1],
                      sq_recv.at[hop - 1], m, s - (hop if hop <= 2 else 2))

    for hop in PART_HOPS[:2]:
        gr_arrived(PART_HOPS.index(hop))

        @pl.when(s >= hop)
        def _(hop=hop):
            seq_send[hop - 1] = total(hop).astype(jnp.bfloat16)
            sq_copy(hop).start()
    for hop in PART_HOPS[2:4]:
        gr_arrived(PART_HOPS.index(hop))
        grad_own[hop] = total(hop)

        @pl.when((s >= hop) & (s < seq_count - 2))
        def _(hop=hop):
            sq_copy(hop + 2).wait_recv()
            grad_own[hop] = grad_own[hop] + seq_recv[hop + 1].astype(jnp.float32)

        @pl.when(s >= hop)
        def _(hop=hop):
            seq_send[hop - 1] = grad_own[hop].astype(jnp.bfloat16)
            sq_copy(hop).start()
    gr_arrived(4)
    grad_own[0] = total(0)
    for hop in (2, 1):
        @pl.when(s < seq_count - hop)
        def _(hop=hop):
            sq_copy(hop).wait_recv()
            grad_own[0] = grad_own[0] + seq_recv[hop - 1].astype(jnp.float32)
    dk_ref[...] = grad_own[0, 0:DH, :].T
    dv_ref[...] = grad_own[0, DH:, :].T

    for slot in (0, 1, 2, 3):
        store(slot, 0).wait()
        store(slot, 1).wait()
    for hop in (1, 2):
        @pl.when(s < seq_count - hop)
        def _(hop=hop):
            kv_seq(0, hop).wait_send()

        @pl.when((s >= hop) & (s < seq_count - 2))
        def _(hop=hop):
            kv_seq(hop, hop + 2).wait_send()
    for slot in (1, 2, 3):
        for hop in range(HOPS):
            kv_head(slot, hop).wait_send()
        for part in range(len(PARTS)):
            gr_copy(slot, part).wait_send()
    for hop in range(1, HOPS):
        @pl.when(s >= hop)
        def _(hop=hop):
            sq_copy(hop).wait_send()


def hand_over(a, b, c, d, a_out, b_out, c_out, d_out, a_on, b_on, c_on, d_on, in_sem, out_sem):
    loads, stores = [], []
    for at, (src, on, dst) in enumerate(
            ((a, a_on, a_out), (b, b_on, b_out), (c, c_on, c_out), (d, d_on, d_out))):
        pieces = PIECES if len(src.shape) == 3 else 1
        size = src.shape[-2] // pieces
        for n in range(pieces):
            part = pl.ds(n * size, size)
            part = (0, part) if len(src.shape) == 3 else (part,)
            loads.append(pltpu.make_async_copy(src.at[part], on.at[part], in_sem.at[at, n]))
            stores.append(pltpu.make_async_copy(on.at[part], dst.at[part], out_sem.at[at, n]))
    for load in loads:
        load.start()
    for load, store in zip(loads, stores):
        load.wait()
        store.start()
    for store in stores:
        store.wait()


def shards(queries, trunk_keys, trunk_values, out_grad, segment_ids):
    rows = trunk_keys.shape[0]
    width = queries.shape[2]
    heads = lax.axis_size("head")
    seq_count = lax.axis_size("seq")
    group_size = width // (DH * heads)
    slab = group_size * DH
    vmem = pl.BlockSpec(memory_space=pltpu.VMEM)
    hbm = pl.BlockSpec(memory_space=pltpu.HBM)
    free = pl.BlockSpec(memory_space=pl.ANY)
    bf16, f32 = jnp.bfloat16, jnp.float32
    dma = pltpu.SemaphoreType.DMA
    big = jax.ShapeDtypeStruct(queries.shape, bf16)
    small = jax.ShapeDtypeStruct(trunk_keys.shape, f32)
    results = pl.pallas_call(
        functools.partial(kernel, seq_count, heads, group_size),
        out_shape=(big, big, small, small),
        in_specs=[hbm] * 5,
        out_specs=(free, free, vmem, vmem),
        scratch_shapes=[
            pltpu.VMEM((1, rows), jnp.int32),
            pltpu.VMEM((heads, HOPS, 2 * rows + 16, DH), bf16),
            pltpu.VMEM((heads, rows, slab), bf16),
            pltpu.VMEM((heads, rows, slab), bf16),
            pltpu.VMEM((heads, rows, slab), bf16),
            pltpu.VMEM((heads, rows, slab), bf16),
            pltpu.VMEM((HOPS * rows, DH), bf16),
            pltpu.VMEM((HOPS * rows, DH), bf16),
            pltpu.VMEM((rows, SPAN * rows), f32),
            pltpu.VMEM((group_size * rows, HOPS * rows), bf16),
            pltpu.VMEM((group_size * rows, HOPS * rows), bf16),
            pltpu.VMEM((HOPS, 2 * DH, rows), f32),
            pltpu.VMEM((3, HOPS, 2 * DH, rows), bf16),
            pltpu.VMEM((3, HOPS, 2 * DH, rows), bf16),
            pltpu.VMEM((SPAN, 2 * DH, rows), bf16),
            pltpu.VMEM((SPAN, 2 * DH, rows), bf16),
            dma((3,)), dma((2, heads)), dma((2, heads)),
            dma((heads, HOPS)), dma((HOPS,)), dma((heads, HOPS)),
            dma((3, len(PARTS))), dma((3, len(PARTS))), dma((SPAN,)), dma((SPAN,)),
        ],
        compiler_params=pltpu.CompilerParams(
            collective_id=0, has_side_effects=True, vmem_limit_bytes=62 * 1024 * 1024),
        cost_estimate=pl.CostEstimate(
            flops=12 * rows * rows * HOPS * width, bytes_accessed=8 * rows * width,
            transcendentals=rows * rows * HOPS * width // DH),
    )(queries, trunk_keys, trunk_values, out_grad, segment_ids.reshape(1, rows))
    return tuple(pl.pallas_call(
        hand_over,
        out_shape=(big, big, small, small),
        in_specs=[free] * 4,
        out_specs=(free,) * 4,
        scratch_shapes=[
            pltpu.VMEM(big.shape, bf16), pltpu.VMEM(big.shape, bf16),
            pltpu.VMEM(small.shape, f32), pltpu.VMEM(small.shape, f32),
            dma((4, PIECES)), dma((4, PIECES)),
        ],
        compiler_params=pltpu.CompilerParams(vmem_limit_bytes=62 * 1024 * 1024),
    )(*results))


def solution(mesh):
    placed = (
        P("head", "seq", None),
        P("seq", "head"),
        P("seq", "head"),
        P("head", "seq", None),
        P("seq"),
    )
    return jax.shard_map(
        shards,
        mesh=mesh,
        in_specs=placed,
        out_specs=(
            P("head", "seq", None),
            P("head", "seq", None),
            P("seq", "head"),
            P("seq", "head"),
        ),
        check_vma=False,
    )
```
